32 devices in a mesh: section: 4 (over y, core), dp: 4 (over z), tensor: 2 (over x).
Axes of the slice: x: 2, y: 2, z: 4, core: 2. Of those that a mesh axis runs over, the one named last changes fastest.
Arguments:
- hidden_in: bfloat16 [1024, 5120], P('dp', 'tensor'), may hold values from -6 to 6
- kv_cache: bfloat16 [4, 4, 2, 1024, 512], P('section', 'dp', None, None, 'tensor'), may hold values from -512 to 512
- norm_gain: float32 [4, 5120], P('section'), may hold values from 0.25 to 1.75
- w_query: bfloat16 [4, 5120, 2560], P('section', 'dp', 'tensor'), may hold values from -0.078125 to 0.078125
- w_keyval: bfloat16 [4, 5120, 2, 512], P('section', 'dp', None, 'tensor'), may hold values from -0.078125 to 0.078125
- w_out: bfloat16 [4, 2560, 5120], P('section', 'tensor', 'dp'), may hold values from -1.1953125 to 1.1953125
- stretch_count: int32 [4], P('dp'), may hold values from 1 to 2, 6 in all
- prefix_len: int32 [4], P('dp'), may hold values from 1 to 1024, 2560 in all
Outputs:
- attn_out: bfloat16 [4, 1024, 5120], P('section', 'dp', 'tensor')
- hidden_out: bfloat16 [4, 1024, 5120], P('section', 'dp', 'tensor')
The draws below stay inside these ranges and needn't reach their ends.
Inputs may be any that keep to these rules, and one draw needn't show every extreme that they name: `stretch_count`: some transcript has 2 live stretches. `prefix_len`: some transcript keeps 1024 rows.
All inputs are finite; a program needn't handle non-finite values. No bound on the sum of `stretch_count` or of `prefix_len` on one device may be relied on, other than what follows from the above.
Results may differ from the reference program's by a relative error of at most 0.02.
Values may be sent and summed in bfloat16 or wider, within the bound.
A program may use at most 128 MiB of HBM per device.

```python
import math
import jax
import jax.numpy as jnp
import numpy as np
from jax import lax

D = 5120
HEADS = 20
KV_HEADS = 4
HEAD_DIM = 128
STRETCH = 128
SLOTS = 2
PREFIX = 1024
GROUPS = 4
N_SECTION = 4
N_TENSOR = 2


def draw_kv_cache(key, part):
    rand_keys = jax.random.split(key, 6)
    full_shape = (N_SECTION, GROUPS, 2, PREFIX, KV_HEADS * HEAD_DIM)
    section_index = jnp.arange(N_SECTION, dtype=jnp.int32)[:, None, None, None]
    bulk_draw = jax.random.truncated_normal(rand_keys[0], -6.0, 6.0, full_shape, jnp.float32)
    strength = jnp.exp(jax.random.uniform(rand_keys[1], (N_SECTION, GROUPS, 1, 1), jnp.float32, math.log(40.0), math.log(160.0)))
    drawn = jnp.exp(jax.random.uniform(rand_keys[5], (N_SECTION, GROUPS, 1, 1), jnp.float32, math.log(2.0), math.log(4.0)))
    strength = jnp.where(section_index == 0, strength, drawn)
    head_pick = jax.random.randint(rand_keys[2], (N_SECTION, GROUPS, 1, 1), 0, KV_HEADS)
    lead_dir = jax.random.truncated_normal(rand_keys[3], -3.0, 3.0, (N_SECTION, GROUPS, 2, HEAD_DIM), jnp.float32)
    nudge_dir = 2.0 * jax.random.truncated_normal(rand_keys[4], -3.0, 3.0, (N_SECTION, GROUPS, 2, HEAD_DIM), jnp.float32)
    level_mult = jnp.array([1.0, 0.4], jnp.float32)
    strong_rows = strength * level_mult[None, None, :, None] * lead_dir
    special_rows = jnp.stack([strong_rows[:, :, 0], strong_rows[:, :, 0] + nudge_dir[:, :, 0], strong_rows[:, :, 1], strong_rows[:, :, 1] + nudge_dir[:, :, 1]], axis=2)
    special_rows = jnp.tile(special_rows, (1, 1, 1, KV_HEADS))
    special_rows = jnp.concatenate([special_rows, jnp.zeros((N_SECTION, GROUPS, PREFIX - 4, KV_HEADS * HEAD_DIM), jnp.float32)], axis=2)
    row_index = jnp.arange(PREFIX, dtype=jnp.int32)[None, None, :, None]
    col_index = jnp.arange(KV_HEADS * HEAD_DIM, dtype=jnp.int32)[None, None, None, :]
    head_index = col_index // HEAD_DIM
    chosen_cells = (row_index < 4) & (head_index == head_pick)
    key_plane = jnp.clip(jnp.where(chosen_cells, special_rows, bulk_draw[:, :, 0]), -512.0, 512.0)
    group_index = jnp.arange(GROUPS, dtype=jnp.int32)[None, :, None, None]
    corner_block = (section_index == 0) & (group_index == 0)
    top_col = head_pick[0, 0, 0, 0] * HEAD_DIM
    key_plane = jnp.where(corner_block & (row_index == 0) & (col_index == top_col), 512.0, key_plane)
    key_plane = jnp.where(corner_block & (row_index == 2) & (col_index == top_col + 1), -512.0, key_plane)
    result = jnp.stack([key_plane, bulk_draw[:, :, 1]], axis=2)
    return result.astype(jnp.bfloat16)


def block_levels(key, dims, cuts, low, top_value):
    def one(dim, parts):
        draws = jax.random.uniform(jax.random.fold_in(jax.random.fold_in(key, 6), dim), (parts,), jnp.float32, low / len(cuts), top_value / len(cuts))
        return jnp.repeat(jnp.exp(draws), dims[dim] // parts).reshape((-1,) + (1,) * (len(dims) - dim - 1))

    level = one(*cuts[0])
    for cut in cuts[1:]:
        level = level * one(*cut)
    return level


def split_up(amount, total, limit, slope):
    loads = [(1 << 20) // math.isqrt(grade ** slope) + 1 for grade in range(2, amount + 1)]
    surplus, given = total - limit - (amount - 1), [1] * (amount - 1)
    while surplus > 0:
        movable = [i for i in range(amount - 1) if given[i] < limit]
        pool, budget = sum([loads[i] for i in movable]), surplus
        for i in movable:
            addition = min(limit - given[i], max(1, budget * loads[i] // pool), surplus)
            given[i] = given[i] + addition
            surplus = surplus - addition
    return np.array([limit] + given)


def uneven_parts(own_key, count, total, bound, slope):
    if count == 2:
        one = jax.random.randint(own_key, (), max(1, total - bound), min(bound, total - 1) + 1)
        return jnp.stack([one, total - one])
    tallies = jnp.asarray(split_up(count, total, bound, slope), jnp.int32)
    pairs = (count - 1) // 2
    giver, sink = tallies[1:1 + 2 * pairs:2], tallies[2:2 + 2 * pairs:2]
    slack = jnp.minimum(giver - 1, bound - sink)
    passed = jax.random.randint(jax.random.fold_in(own_key, 1), (pairs,), 0, 1 << 20) % (slack + 1)
    tallies = tallies.at[1:1 + 2 * pairs:2].set(giver - passed).at[2:2 + 2 * pairs:2].set(sink + passed)
    return tallies[jax.random.permutation(jax.random.fold_in(own_key, 2), count)]


def bell_draw(rng, shape, width, bound, cuts=(), held_as=jnp.bfloat16):
    factor_of = block_levels(rng, shape, cuts, -0.22, 0.18) if cuts else 1.0
    drawn = jax.random.normal(rng, shape, jnp.float32) * width * factor_of
    return jnp.minimum(jnp.maximum(drawn, -bound), bound).astype(held_as)


def setup_inputs(seed: int = 0) -> dict:
    streams_of = jax.random.split(jax.random.key(seed), 9)
    return {
        "hidden_in": bell_draw(streams_of[0], (GROUPS * SLOTS * STRETCH, D), 1.0, 6.0, ((0, 4), (1, 2))),
        "kv_cache": draw_kv_cache(jax.random.fold_in(streams_of[8], 71), 0),
        "norm_gain": jnp.clip(1.0 + 0.15 * jax.random.normal(streams_of[2], (N_SECTION, D), jnp.float32), 0.25, 1.75),
        "w_query": bell_draw(streams_of[3], (N_SECTION, D, HEADS * HEAD_DIM), D ** -0.5, 0.078125, ((0, 4), (1, 4), (2, 2))),
        "w_keyval": bell_draw(streams_of[4], (N_SECTION, D, 2, KV_HEADS * HEAD_DIM), D ** -0.5, 0.078125, ((0, 4), (1, 4), (3, 2))),
        "w_out": bell_draw(streams_of[5], (N_SECTION, HEADS * HEAD_DIM, D), 0.2, 1.1953125, ((0, 4), (1, 2), (2, 4))),
        "stretch_count": uneven_parts(streams_of[6], GROUPS, GROUPS * (SLOTS + 1) // 2, SLOTS, 2).astype(jnp.int32),
        "prefix_len": uneven_parts(streams_of[7], GROUPS, (GROUPS + 1) * PREFIX // 2, PREFIX, 1).astype(jnp.int32),
    }


theta_base = 1000000.0
eps_norm = 1e-06
masked_score = -1e+30

def rotary(values, positions):
    half_dim = values.shape[-1] // 2
    inv_freq = theta_base ** (-(jnp.arange(half_dim, dtype=jnp.float32) * 2.0 / values.shape[-1]))
    angles = positions.astype(jnp.float32)[:, None] * inv_freq[None, :]
    cosine = jnp.cos(angles)[:, None, :]
    sine_part = jnp.sin(angles)[:, None, :]
    first_half = values[..., :half_dim]
    second_half = values[..., half_dim:]
    return jnp.concatenate([first_half * cosine - second_half * sine_part, second_half * cosine + first_half * sine_part], axis=-1)

def group_layer(x_group, kv_store, prefix, gain_vec, query_w, keyval_w, out_w):
    row_total = x_group.shape[0]
    x_float = x_group.astype(jnp.float32)
    normed = (x_float * lax.rsqrt(lax.optimization_barrier(jnp.mean(x_float * x_float, axis=1, keepdims=True)) + eps_norm) * gain_vec[None, :]).astype(jnp.bfloat16)
    positions = prefix + jnp.arange(row_total, dtype=jnp.int32)
    query_vec = jnp.dot(normed, query_w, preferred_element_type=jnp.float32).reshape(row_total, HEADS, HEAD_DIM)
    query_vec = rotary(query_vec, positions)
    keyval = jnp.dot(normed, keyval_w.reshape(D, 2 * KV_HEADS * HEAD_DIM), preferred_element_type=jnp.float32)
    key_new = rotary(keyval[:, :KV_HEADS * HEAD_DIM].reshape(row_total, KV_HEADS, HEAD_DIM), positions).astype(jnp.bfloat16)
    value_new = keyval[:, KV_HEADS * HEAD_DIM:].reshape(row_total, KV_HEADS, HEAD_DIM).astype(jnp.bfloat16)
    all_keys = jnp.concatenate([kv_store[0].reshape(PREFIX, KV_HEADS, HEAD_DIM), key_new], axis=0)
    all_vals = jnp.concatenate([kv_store[1].reshape(PREFIX, KV_HEADS, HEAD_DIM), value_new], axis=0)
    group_size = HEADS // KV_HEADS
    query_grp = query_vec.reshape(row_total, KV_HEADS, group_size, HEAD_DIM).astype(jnp.float32)
    scores = jnp.einsum('rkgd,jkd->kgrj', query_grp, all_keys.astype(jnp.float32), precision=lax.Precision.HIGHEST) * HEAD_DIM ** (-0.5)
    key_pos = jnp.arange(PREFIX + row_total, dtype=jnp.int32)
    row_pos = jnp.arange(row_total, dtype=jnp.int32)
    allowed = jnp.where(key_pos[None, :] < PREFIX, (key_pos < prefix)[None, :], key_pos[None, :] - PREFIX <= row_pos[:, None])
    scores = jnp.where(allowed[None, None], scores, masked_score)
    row_max = lax.optimization_barrier(jnp.max(scores, axis=-1, keepdims=True))
    expd = jnp.exp(scores - row_max)
    probs = (expd / lax.optimization_barrier(jnp.sum(expd, axis=-1, keepdims=True))).astype(jnp.bfloat16)
    mixed_heads = jnp.einsum('kgrj,jkd->rkgd', probs.astype(jnp.float32), all_vals.astype(jnp.float32))
    mixed_heads = mixed_heads.reshape(row_total, HEADS * HEAD_DIM).astype(jnp.bfloat16)
    local_cols = HEADS * HEAD_DIM // N_TENSOR
    partials = jnp.einsum('rtc,tcd->trd', mixed_heads.reshape(row_total, N_TENSOR, local_cols).astype(jnp.float32), out_w.reshape(N_TENSOR, local_cols, D).astype(jnp.float32))
    rounded = lax.optimization_barrier(partials.astype(jnp.bfloat16))
    attn = lax.optimization_barrier(jnp.sum(rounded.astype(jnp.float32), axis=0))
    return (attn.astype(jnp.bfloat16), (x_float + attn).astype(jnp.bfloat16))

def reference(hidden_in, kv_cache, norm_gain, w_query, w_keyval, w_out, stretch_count, prefix_len):
    row_total = SLOTS * STRETCH
    x_now = hidden_in.reshape(GROUPS, row_total, D)
    live_mask = ((jnp.arange(row_total, dtype=jnp.int32) // STRETCH)[None, :] < stretch_count[:, None])[:, :, None]
    attn_list = []
    hidden_list = []
    for section_num in range(N_SECTION):

        def per_group(items, section_num=section_num):
            x_group, kv_store, prefix = items
            return group_layer(x_group, kv_store, prefix, norm_gain[section_num], w_query[section_num], w_keyval[section_num], w_out[section_num])
        attn_vals, hid_vals = lax.map(per_group, (x_now, kv_cache[section_num], prefix_len))
        attn_list.append(jnp.where(live_mask, attn_vals, jnp.zeros_like(attn_vals)).reshape(GROUPS * row_total, D))
        hidden_list.append(jnp.where(live_mask, hid_vals, jnp.zeros_like(hid_vals)).reshape(GROUPS * row_total, D))
        x_now = hid_vals
    return (jnp.stack(attn_list, axis=0), jnp.stack(hidden_list, axis=0))
```

```python
import functools

import jax
import jax.numpy as jnp
from jax import lax
from jax.experimental import pallas as pl
from jax.experimental.pallas import tpu as pltpu
from jax.sharding import PartitionSpec as P

HEAD_DIM = 128
STRETCH = 128


theta_base = 1000000.0
eps_norm = 1e-06
masked_score = -1e30


def from_behind(value, axis, steps):
    count = lax.axis_size(axis)
    leading, last = (max(0, -steps), min(count, count - steps))
    return lax.ppermute(value, axis, [(source, source + steps) for source in range(leading, last)])


def rotary(values, positions):
    half_dim = values.shape[-1] // 2
    inv_freq = theta_base ** (-(jnp.arange(half_dim, dtype=jnp.float32) * 2.0 / values.shape[-1]))
    angles = positions.astype(jnp.float32)[:, None] * inv_freq[None, :]
    cosine = jnp.cos(angles)[:, None, :]
    sine_part = jnp.sin(angles)[:, None, :]
    first_half = values[..., :half_dim]
    second_half = values[..., half_dim:]
    return jnp.concatenate(
        [
            first_half * cosine - second_half * sine_part,
            second_half * cosine + first_half * sine_part,
        ],
        axis=-1,
    )


def shards(hidden_in, kv_cache, norm_gain, w_query, w_keyval, w_out, stretch_count, prefix_len):
    section_idx = lax.axis_index("section")
    section_total = lax.axis_size("section")
    tensor_idx = lax.axis_index("tensor")
    query_w, keyval_w = (
        lax.all_gather(w_query, "dp", axis=1, tiled=True),
        lax.all_gather(w_keyval, "dp", axis=1, tiled=True),
    )
    out_w = lax.all_gather(w_out, "dp", axis=2, tiled=True)[0]
    query_w = query_w[0]
    width = query_w.shape[0]
    local_cols = query_w.shape[1]
    keyval_w = keyval_w[0].reshape(width, -1)
    gain_vec = norm_gain[0]
    kv_store = kv_cache[0, 0]
    live_count = stretch_count[0]
    prefix = prefix_len[0]
    rows_all = hidden_in.shape[0]
    slot_total = rows_all // STRETCH
    part_width = hidden_in.shape[1]
    kv_width = kv_store.shape[2]
    kv_local = kv_width // HEAD_DIM
    heads_local = local_cols // HEAD_DIM
    group_size = heads_local // kv_local
    prefix_cap = kv_store.shape[1]
    key_block = min(prefix_cap, 512)
    block_total = prefix_cap // key_block
    score_scale = HEAD_DIM ** (-0.5)
    tick_total = slot_total + section_total - 1
    full_prec = lax.Precision.HIGHEST
    key_buf = jnp.zeros((rows_all, kv_width), jnp.bfloat16)
    value_buf = jnp.zeros((rows_all, kv_width), jnp.bfloat16)
    attn_buf = jnp.zeros((rows_all, part_width), jnp.bfloat16)
    hid_buf = jnp.zeros((rows_all, part_width), jnp.bfloat16)
    inputs_all = lax.all_gather(hidden_in, "tensor", axis=1, tiled=True)
    incoming = jnp.zeros((STRETCH, width), jnp.bfloat16)
    for tick_num in range(tick_total):
        slot_num = tick_num - section_idx
        valid = (slot_num >= 0) & (slot_num < slot_total)
        slot_safe = jnp.clip(slot_num, 0, slot_total - 1)
        row_start = slot_safe * STRETCH
        first_rows = lax.dynamic_slice_in_dim(inputs_all, row_start, STRETCH, 0)
        x_full = jnp.where(section_idx == 0, first_rows, incoming)
        x_part = lax.dynamic_slice_in_dim(x_full, tensor_idx * part_width, part_width, 1)
        x_float = x_full.astype(jnp.float32)
        normed = (
            x_float
            * lax.rsqrt(jnp.mean(x_float * x_float, axis=1, keepdims=True) + eps_norm)
            * gain_vec[None, :]
        ).astype(jnp.bfloat16)
        positions = prefix + row_start + jnp.arange(STRETCH, dtype=jnp.int32)
        query_vec = jnp.dot(normed, query_w, preferred_element_type=jnp.float32).reshape(
            STRETCH, heads_local, HEAD_DIM
        )
        query_vec = rotary(query_vec, positions)
        keyval = jnp.dot(normed, keyval_w, preferred_element_type=jnp.float32)
        key_new = (
            rotary(keyval[:, :kv_width].reshape(STRETCH, kv_local, HEAD_DIM), positions)
            .astype(jnp.bfloat16)
            .reshape(STRETCH, kv_width)
        )
        value_new = keyval[:, kv_width:].astype(jnp.bfloat16)
        key_upd = lax.dynamic_update_slice(key_buf, key_new, (row_start, 0))
        value_upd = lax.dynamic_update_slice(value_buf, value_new, (row_start, 0))
        key_buf = jnp.where(valid, key_upd, key_buf)
        value_buf = jnp.where(valid, value_upd, value_buf)
        query_rows = (
            query_vec.reshape(STRETCH, kv_local, group_size, HEAD_DIM)
            .transpose(1, 0, 2, 3)
            .reshape(kv_local, STRETCH * group_size, HEAD_DIM)
        )
        row_of = row_start + jnp.arange(STRETCH * group_size, dtype=jnp.int32) // group_size
        new_keys = (
            key_upd.reshape(rows_all, kv_local, HEAD_DIM).transpose(1, 0, 2).astype(jnp.float32)
        )
        new_vals = value_upd.reshape(rows_all, kv_local, HEAD_DIM).transpose(1, 0, 2)
        new_scores = (
            jnp.einsum("kqd,kjd->kqj", query_rows, new_keys, precision=full_prec) * score_scale
        )
        new_ok = jnp.arange(rows_all, dtype=jnp.int32)[None, :] <= row_of[:, None]
        new_scores = jnp.where(new_ok[None], new_scores, masked_score)

        def kept_scores(blk_idx):
            blk_start = blk_idx * key_block
            key_tile = (
                lax.dynamic_slice_in_dim(kv_store[0], blk_start, key_block, 0)
                .reshape(key_block, kv_local, HEAD_DIM)
                .transpose(1, 0, 2)
                .astype(jnp.float32)
            )
            scores = (
                jnp.einsum("kqd,kjd->kqj", query_rows, key_tile, precision=full_prec) * score_scale
            )
            key_ok = blk_start + jnp.arange(key_block, dtype=jnp.int32) < prefix
            return jnp.where(key_ok[None, None, :], scores, masked_score)

        row_max = jnp.max(new_scores, axis=-1)
        row_sum = jnp.sum(jnp.exp(new_scores - row_max[..., None]), axis=-1)

        def stat_step(blk_idx, carry):
            run_max, run_sum = carry
            scores = kept_scores(blk_idx)
            next_max = jnp.maximum(run_max, jnp.max(scores, axis=-1))
            next_sum = run_sum * jnp.exp(run_max - next_max) + jnp.sum(
                jnp.exp(scores - next_max[..., None]), axis=-1
            )
            return (next_max, next_sum)

        row_max, row_sum = lax.fori_loop(0, block_total, stat_step, (row_max, row_sum))
        new_probs = (jnp.exp(new_scores - row_max[..., None]) / row_sum[..., None]).astype(
            jnp.bfloat16
        )
        weighted = jnp.einsum(
            "kqj,kjd->kqd", new_probs, new_vals, preferred_element_type=jnp.float32
        )

        def value_step(blk_idx, total):
            scores = kept_scores(blk_idx)
            probs = (jnp.exp(scores - row_max[..., None]) / row_sum[..., None]).astype(jnp.bfloat16)
            value_tile = (
                lax.dynamic_slice_in_dim(kv_store[1], blk_idx * key_block, key_block, 0)
                .reshape(key_block, kv_local, HEAD_DIM)
                .transpose(1, 0, 2)
            )
            return total + jnp.einsum(
                "kqj,kjd->kqd", probs, value_tile, preferred_element_type=jnp.float32
            )

        weighted = lax.fori_loop(0, block_total, value_step, weighted)
        mixed_heads = (
            weighted.reshape(kv_local, STRETCH, group_size, HEAD_DIM)
            .transpose(1, 0, 2, 3)
            .reshape(STRETCH, local_cols)
            .astype(jnp.bfloat16)
        )
        partials = jnp.dot(mixed_heads, out_w, preferred_element_type=jnp.float32)
        attn_part = lax.psum_scatter(
            partials.astype(jnp.bfloat16), "tensor", scatter_dimension=1, tiled=True
        ).astype(jnp.float32)
        hid_part = (x_part.astype(jnp.float32) + attn_part).astype(jnp.bfloat16)
        live_now = valid & (slot_num < live_count)
        attn_vals = jnp.where(live_now, attn_part.astype(jnp.bfloat16), jnp.zeros_like(hid_part))
        hid_vals = jnp.where(live_now, hid_part, jnp.zeros_like(hid_part))
        attn_buf = jnp.where(
            valid, lax.dynamic_update_slice(attn_buf, attn_vals, (row_start, 0)), attn_buf
        )
        hid_buf = jnp.where(
            valid, lax.dynamic_update_slice(hid_buf, hid_vals, (row_start, 0)), hid_buf
        )
        if tick_num + 1 < tick_total:
            joined = lax.all_gather(hid_part, "tensor", axis=1, tiled=True)
            incoming = from_behind(joined, "section", 1)
    return (attn_buf[None], hid_buf[None])


def relay_kernel(
    slots, sections, groups, tensors,
    x_in, wqkv_q, wqkv_kv, w_out, gain, kv, cos_ref, sin_ref, bias_ref,
    attn_ref, hid_ref,
    xbuf, q_send, q_recv, ss_send, ss_recv, q_own, q_cat, k_all, v_all,
    heads, p_send, p_recv, x_next, a_send, a_recv, h_recv, h_send,
    xin_s, x_r, q_s, q_r, ss_s, ss_r, h_s, h_r, p_s, p_r, xn_s, a_s, a_r, hc_s, hc_r, loc,
):
    s = lax.axis_index("section")
    g = lax.axis_index("dp")
    t = lax.axis_index("tensor")
    last = sections - 1
    per_t = groups // tensors
    width = x_next.shape[-1]
    q_cols = wqkv_q.shape[1]
    kv_cols = kv.shape[2]
    kv_heads = kv_cols // HEAD_DIM
    head_total = q_cols // HEAD_DIM
    group_size = head_total // kv_heads
    kept = kv.shape[1]
    half_cols = group_size * HEAD_DIM

    def dev(sec, grp, ten):
        return {"section": sec, "dp": grp, "tensor": ten}

    def remote(src, dst, send, recv, target):
        return pltpu.make_async_remote_copy(
            src_ref=src, dst_ref=dst, send_sem=send, recv_sem=recv,
            device_id=target, device_id_type=pl.DeviceIdType.MESH,
        )

    barrier = pltpu.get_barrier_semaphore()
    for dg in range(groups):
        for dt in range(tensors):
            if dg or dt:
                pl.semaphore_signal(
                    barrier, inc=1,
                    device_id=dev(s, lax.rem(g + dg, groups), lax.rem(t + dt, tensors)),
                    device_id_type=pl.DeviceIdType.MESH,
                )

    @pl.when(s > 0)
    def _():
        pl.semaphore_signal(
            barrier, inc=1, device_id=dev(s - 1, g, t), device_id_type=pl.DeviceIdType.MESH
        )

    @pl.when(s < last)
    def _():
        pl.semaphore_signal(
            barrier, inc=1, device_id=dev(s + 1, g, t), device_id_type=pl.DeviceIdType.MESH
        )

    edge = jnp.where(s > 0, 1, 0) + jnp.where(s < last, 1, 0)
    pl.semaphore_wait(barrier, groups * tensors - 1 + edge)

    def input_copy(j, c, td):
        return remote(
            x_in.at[pl.ds(j * STRETCH, STRETCH), pl.ds(c * width, width)],
            xbuf.at[j, g], xin_s.at[j, c, td], x_r.at[j, g], dev(0, per_t * t + c, td),
        )

    def local_copy(j, c):
        return pltpu.make_async_copy(
            x_in.at[pl.ds(j * STRETCH, STRETCH), pl.ds(c * width, width)], xbuf.at[j, g], loc.at[j]
        )

    def for_inputs(do):
        for j in range(slots):
            for c in range(per_t):
                for td in range(tensors):
                    own = (per_t * t + c == g) & (td == t)

                    @pl.when((s == 0) & jnp.logical_not(own))
                    def _():
                        do(input_copy(j, c, td))

    for_inputs(lambda copy: copy.start())
    is_local = (s == 0) & (g // per_t == t)
    for j in range(slots):
        for c in range(per_t):

            @pl.when((s == 0) & (per_t * t + c == g))
            def _():
                local_copy(j, c).start()

    for h in range(kv_heads):
        piece = kv[0, :, h * HEAD_DIM : (h + 1) * HEAD_DIM]
        k_all[h, :kept, :HEAD_DIM] = piece
        k_all[h, :kept, HEAD_DIM:] = piece
        v_all[h, :kept, :] = kv[1, :, h * HEAD_DIM : (h + 1) * HEAD_DIM]
        fresh = k_all.shape[1] - kept
        k_all[h, kept:, :] = jnp.zeros((fresh, 2 * HEAD_DIM), jnp.bfloat16)
        v_all[h, kept:, :] = jnp.zeros((fresh, HEAD_DIM), jnp.bfloat16)
    for j in range(slots):
        for c in range(per_t):

            @pl.when((s == 0) & (per_t * t + c == g))
            def _():
                local_copy(j, c).wait()

    def q_copy(j, src, dst_slot, sem, target):
        return remote(q_send.at[j, src], q_recv.at[j, dst_slot], q_s.at[j, src], q_r.at[j, sem], target)

    def ss_copy(j, src, dst_slot, sem, target):
        return remote(
            ss_send.at[j, src], ss_recv.at[j, dst_slot], ss_s.at[j, src], ss_r.at[j, sem], target
        )

    def h_copy(j, part, slot, peer):
        cols = pl.ds(part * half_cols, half_cols)
        return remote(
            heads.at[j, slot, :, cols], heads.at[j, slot, :, cols],
            h_s.at[j, peer, part], h_r.at[j, slot, part], dev(s, peer, t),
        )

    def p_copy(j, tr):
        return remote(
            p_send.at[j, tr], p_recv.at[j, tr], p_s.at[j, tr], p_r.at[j, tr],
            dev(s, g, lax.rem(t + 1, tensors)),
        )

    def x_copy(j, tr, sec):
        return remote(x_next.at[j, tr], xbuf.at[j, tr], xn_s.at[j, tr], x_r.at[j, tr], dev(sec, g, t))

    def a_copy(j, tr, c, peer):
        return remote(a_send.at[j, tr], a_recv.at[j, c], a_s.at[j, tr], a_r.at[j, c], dev(s, peer, t))

    def hc_copy(j, sec):
        return remote(h_send.at[j], h_recv.at[j], hc_s.at[j], hc_r.at[j], dev(sec, g, t))

    def rotate(values, cosine, sine):
        return values * cosine + pltpu.roll(values, HEAD_DIM // 2, 1) * sine

    @pl.loop(0, slots)
    def _(j):
        row = pl.multiple_of(j * STRETCH, STRETCH)
        for k in (2, 1, 3, 0) if groups == 4 else list(range(1, groups)) + [0]:
            d = lax.rem(g + k, groups)
            arrives = jnp.logical_not(is_local) | (d != g)

            @pl.when(arrives)
            def _():
                x_copy(j, d, s).wait_recv()

            x_val = xbuf[j, d].astype(jnp.float32)
            square = jnp.sum(x_val * x_val, axis=1, keepdims=True)
            ss_send[j, d] = jnp.broadcast_to(square, (STRETCH, HEAD_DIM))
            x_gain = (x_val * gain[...]).astype(jnp.bfloat16)
            part_q = jnp.dot(x_gain, wqkv_q[...], preferred_element_type=jnp.float32)
            part_kv = jnp.dot(x_gain, wqkv_kv[...], preferred_element_type=jnp.float32)
            if k:
                q_send[j, d, :, :q_cols] = part_q.astype(jnp.bfloat16)
                q_send[j, d, :, q_cols:] = part_kv.astype(jnp.bfloat16)
                ss_copy(j, d, g, g, dev(s, d, t)).start()
                q_copy(j, d, g, g, dev(s, d, t)).start()
            else:
                q_own[:, :q_cols] = part_q
                q_own[:, q_cols:] = part_kv
        square = ss_send[j, g]
        for k in range(1, groups):
            src = lax.rem(g + k, groups)
            ss_copy(j, src, src, src, dev(s, src, t)).wait_recv()
            q_copy(j, src, src, src, dev(s, src, t)).wait_recv()
            square = square + ss_recv[j, src]
        scale = lax.rsqrt(square * (1.0 / (groups * width)) + eps_norm)
        cosine = cos_ref[pl.ds(row, STRETCH), :]
        sine = sin_ref[pl.ds(row, STRETCH), :]

        def total(col):
            value = q_own[:, col : col + HEAD_DIM]
            for k in range(1, groups):
                src = lax.rem(g + k, groups)
                value = value + q_recv[j, src, :, col : col + HEAD_DIM].astype(jnp.float32)
            return value * scale

        for h in range(kv_heads):
            fresh = pl.ds(pl.multiple_of(kept + row, STRETCH), STRETCH)
            key_new = rotate(total(q_cols + h * HEAD_DIM), cosine, sine).astype(jnp.bfloat16)
            k_all[h, fresh, :HEAD_DIM] = key_new
            k_all[h, fresh, HEAD_DIM:] = key_new
            v_all[h, fresh, :] = total(q_cols + kv_cols + h * HEAD_DIM).astype(jnp.bfloat16)
        for h in range(head_total):
            query = rotate(total(h * HEAD_DIM), cosine, sine) * HEAD_DIM ** (-0.5)
            high = query.astype(jnp.bfloat16)
            q_cat[h, :, :HEAD_DIM] = high
            q_cat[h, :, HEAD_DIM:] = (query - high.astype(jnp.float32)).astype(jnp.bfloat16)

        for h in range(kv_heads):
            for i in range(group_size):
                n = h * group_size + i
                scores = lax.dot_general(
                    q_cat[n], k_all[h], (((1,), (1,)), ((), ())), preferred_element_type=jnp.float32
                ) + bias_ref[pl.ds(row, STRETCH), :]
                probs = jnp.exp(scores - jnp.max(scores, axis=1, keepdims=True))
                norm = jnp.sum(probs, axis=1, keepdims=True)
                mixed = jnp.dot(
                    probs.astype(jnp.bfloat16), v_all[h], preferred_element_type=jnp.float32
                )
                heads[j, g, :, n * HEAD_DIM : (n + 1) * HEAD_DIM] = (mixed / norm).astype(jnp.bfloat16)
            for k in range(1, groups):
                h_copy(j, h, g, lax.rem(g + k, groups)).start()

        order = (0, 1, 3, 2) if groups == 4 else range(groups)
        for k in order:
            tr = lax.rem(g + k, groups)
            if k:
                for h in range(kv_heads):
                    h_copy(j, h, tr, tr).wait_recv()
            p_send[j, tr] = jnp.dot(
                heads[j, tr], w_out[...], preferred_element_type=jnp.float32
            ).astype(jnp.bfloat16)
            p_copy(j, tr).start()
        for k in order:
            tr = lax.rem(g + k, groups)
            p_copy(j, tr).wait_recv()
            attn = p_send[j, tr].astype(jnp.float32) + p_recv[j, tr].astype(jnp.float32)
            x_next[j, tr] = (xbuf[j, tr].astype(jnp.float32) + attn).astype(jnp.bfloat16)

            @pl.when(s < last)
            def _():
                x_copy(j, tr, s + 1).start()

            a_send[j, tr] = attn.astype(jnp.bfloat16)

            @pl.when(g // per_t == t)
            def _():
                if k:
                    a_copy(j, tr, lax.rem(g, per_t), tr).start()

    @pl.loop(0, slots)
    def _(j):
        rows = pl.ds(pl.multiple_of(j * STRETCH, STRETCH), STRETCH)

        @pl.when(s > 0)
        def _():
            hc_copy(j, s).wait_recv()

        for c in range(per_t):
            cols = slice(c * width, (c + 1) * width)
            owner = per_t * t + c

            @pl.when(owner != g)
            def _():
                a_copy(j, g, c, owner).wait_recv()
                attn_ref[rows, cols] = a_recv[j, c]

            @pl.when(owner == g)
            def _():
                attn_ref[rows, cols] = a_send[j, g]

            @pl.when(s == 0)
            def _():
                h_send[j, :, cols] = (
                    x_in[rows, cols].astype(jnp.float32) + attn_ref[rows, cols].astype(jnp.float32)
                ).astype(jnp.bfloat16)

            @pl.when(s > 0)
            def _():
                h_send[j, :, cols] = (
                    h_recv[j, :, cols].astype(jnp.float32)
                    + attn_ref[rows, cols].astype(jnp.float32)
                ).astype(jnp.bfloat16)

        @pl.when(s < last)
        def _():
            hc_copy(j, s + 1).start()

        hid_ref[rows, :] = h_send[j]

    for_inputs(lambda copy: copy.wait_send())

    @pl.loop(0, slots)
    def _(j):
        for k in range(groups):
            tr = lax.rem(g + k, groups)
            if k:
                q_copy(j, tr, g, g, dev(s, tr, t)).wait_send()
                ss_copy(j, tr, g, g, dev(s, tr, t)).wait_send()
                for h in range(kv_heads):
                    h_copy(j, h, g, tr).wait_send()

                @pl.when(g // per_t == t)
                def _():
                    a_copy(j, tr, lax.rem(g, per_t), tr).wait_send()

            p_copy(j, tr).wait_send()

            @pl.when(s < last)
            def _():
                x_copy(j, tr, s + 1).wait_send()

        @pl.when(s < last)
        def _():
            hc_copy(j, s + 1).wait_send()


def relay_shards(hidden_in, kv_cache, norm_gain, w_query, w_keyval, w_out, stretch_count, prefix_len):
    sections = lax.axis_size("section")
    groups = lax.axis_size("dp")
    tensors = lax.axis_size("tensor")
    width = w_query.shape[1]
    q_cols = w_query.shape[2]
    kv_store = kv_cache[0, 0]
    kept, kv_cols = kv_store.shape[1:]
    kv_heads = kv_cols // HEAD_DIM
    head_total = q_cols // HEAD_DIM
    rows_all = hidden_in.shape[0]
    slots = rows_all // STRETCH
    out_cols = hidden_in.shape[1]
    all_cols = q_cols + 2 * kv_cols
    per_t = groups // tensors
    gain = lax.dynamic_slice_in_dim(norm_gain, lax.axis_index("dp") * width, width, 1)
    prefix = prefix_len[0]
    row_idx = jnp.arange(rows_all, dtype=jnp.int32)
    half_dim = HEAD_DIM // 2
    inv_freq = theta_base ** (-(jnp.arange(half_dim, dtype=jnp.float32) * 2.0 / HEAD_DIM))
    angles = (prefix + row_idx).astype(jnp.float32)[:, None] * inv_freq[None, :]
    cosine, sine = jnp.cos(angles), jnp.sin(angles)
    cos_full = jnp.concatenate([cosine, cosine], axis=1)
    sin_full = jnp.concatenate([-sine, sine], axis=1)
    key_idx = jnp.arange(kept + rows_all, dtype=jnp.int32)[None, :]
    visible = jnp.where(key_idx < kept, key_idx < prefix, key_idx - kept <= row_idx[:, None])
    bias = jnp.where(visible, 0.0, masked_score).astype(jnp.float32)
    vmem = pl.BlockSpec(memory_space=pltpu.VMEM)
    bf16 = jnp.bfloat16
    dma = pltpu.SemaphoreType.DMA
    block = (slots, groups, STRETCH)
    attn, hid = pl.pallas_call(
        functools.partial(relay_kernel, slots, sections, groups, tensors),
        out_shape=[jax.ShapeDtypeStruct((rows_all, out_cols), bf16)] * 2,
        in_specs=[vmem] * 9,
        out_specs=[vmem] * 2,
        scratch_shapes=[
            pltpu.VMEM(block + (width,), bf16),
            pltpu.VMEM(block + (all_cols,), bf16),
            pltpu.VMEM(block + (all_cols,), bf16),
            pltpu.VMEM(block + (HEAD_DIM,), jnp.float32),
            pltpu.VMEM(block + (HEAD_DIM,), jnp.float32),
            pltpu.VMEM((STRETCH, all_cols), jnp.float32),
            pltpu.VMEM((head_total, STRETCH, 2 * HEAD_DIM), bf16),
            pltpu.VMEM((kv_heads, kept + rows_all, 2 * HEAD_DIM), bf16),
            pltpu.VMEM((kv_heads, kept + rows_all, HEAD_DIM), bf16),
            pltpu.VMEM(block + (q_cols,), bf16),
            pltpu.VMEM(block + (width,), bf16),
            pltpu.VMEM(block + (width,), bf16),
            pltpu.VMEM(block + (width,), bf16),
            pltpu.VMEM(block + (width,), bf16),
            pltpu.VMEM((slots, per_t, STRETCH, width), bf16),
            pltpu.VMEM((slots, STRETCH, out_cols), bf16),
            pltpu.VMEM((slots, STRETCH, out_cols), bf16),
            dma((slots, per_t, tensors)),
            dma((slots, groups)),
            dma((slots, groups)),
            dma((slots, groups)),
            dma((slots, groups)),
            dma((slots, groups)),
            dma((slots, groups, kv_heads)),
            dma((slots, groups, kv_heads)),
            dma((slots, groups)),
            dma((slots, groups)),
            dma((slots, groups)),
            dma((slots, groups)),
            dma((slots, per_t)),
            dma((slots,)),
            dma((slots,)),
            dma((slots,)),
        ],
        compiler_params=pltpu.CompilerParams(
            collective_id=0, has_side_effects=True, vmem_limit_bytes=60 * 2**20
        ),
    )(
        hidden_in, w_query[0], w_keyval[0].reshape(width, 2 * kv_cols), w_out[0],
        gain, kv_store, cos_full, sin_full, bias,
    )
    live = (row_idx // STRETCH < stretch_count[0])[:, None]
    return (
        jnp.where(live, attn, jnp.zeros_like(attn))[None],
        jnp.where(live, hid, jnp.zeros_like(hid))[None],
    )


def relay_fits(mesh, width, model_cols):
    return mesh.shape["tensor"] == 2 and width % HEAD_DIM == 0 and model_cols % width == 0


def solution(mesh):
    def either(hidden_in, kv_cache, norm_gain, w_query, *rest):
        fits = relay_fits(mesh, w_query.shape[1], hidden_in.shape[1])
        body = relay_shards if fits else shards
        return body(hidden_in, kv_cache, norm_gain, w_query, *rest)

    return jax.shard_map(
        either,
        mesh=mesh,
        in_specs=(
            P("dp", "tensor"),
            P("section", "dp", None, None, "tensor"),
            P("section", None),
            P("section", "dp", "tensor"),
            P("section", "dp", None, "tensor"),
            P("section", "tensor", "dp"),
            P("dp"),
            P("dp"),
        ),
        out_specs=(P("section", "dp", "tensor"), P("section", "dp", "tensor")),
        check_vma=False,
    )
```

```python
import functools

import jax
import jax.numpy as jnp
from jax import lax
from jax.experimental import pallas as pl
from jax.experimental.pallas import tpu as pltpu
from jax.sharding import PartitionSpec as P

HEAD_DIM = 128
STRETCH = 128


theta_base = 1000000.0
eps_norm = 1e-06
masked_score = -1e30


def from_behind(value, axis, steps):
    count = lax.axis_size(axis)
    leading, last = (max(0, -steps), min(count, count - steps))
    return lax.ppermute(value, axis, [(source, source + steps) for source in range(leading, last)])


def rotary(values, positions):
    half_dim = values.shape[-1] // 2
    inv_freq = theta_base ** (-(jnp.arange(half_dim, dtype=jnp.float32) * 2.0 / values.shape[-1]))
    angles = positions.astype(jnp.float32)[:, None] * inv_freq[None, :]
    cosine = jnp.cos(angles)[:, None, :]
    sine_part = jnp.sin(angles)[:, None, :]
    first_half = values[..., :half_dim]
    second_half = values[..., half_dim:]
    return jnp.concatenate(
        [
            first_half * cosine - second_half * sine_part,
            second_half * cosine + first_half * sine_part,
        ],
        axis=-1,
    )


def shards(hidden_in, kv_cache, norm_gain, w_query, w_keyval, w_out, stretch_count, prefix_len):
    section_idx = lax.axis_index("section")
    section_total = lax.axis_size("section")
    tensor_idx = lax.axis_index("tensor")
    query_w, keyval_w = (
        lax.all_gather(w_query, "dp", axis=1, tiled=True),
        lax.all_gather(w_keyval, "dp", axis=1, tiled=True),
    )
    out_w = lax.all_gather(w_out, "dp", axis=2, tiled=True)[0]
    query_w = query_w[0]
    width = query_w.shape[0]
    local_cols = query_w.shape[1]
    keyval_w = keyval_w[0].reshape(width, -1)
    gain_vec = norm_gain[0]
    kv_store = kv_cache[0, 0]
    live_count = stretch_count[0]
    prefix = prefix_len[0]
    rows_all = hidden_in.shape[0]
    slot_total = rows_all // STRETCH
    part_width = hidden_in.shape[1]
    kv_width = kv_store.shape[2]
    kv_local = kv_width // HEAD_DIM
    heads_local = local_cols // HEAD_DIM
    group_size = heads_local // kv_local
    prefix_cap = kv_store.shape[1]
    key_block = min(prefix_cap, 512)
    block_total = prefix_cap // key_block
    score_scale = HEAD_DIM ** (-0.5)
    tick_total = slot_total + section_total - 1
    full_prec = lax.Precision.HIGHEST
    key_buf = jnp.zeros((rows_all, kv_width), jnp.bfloat16)
    value_buf = jnp.zeros((rows_all, kv_width), jnp.bfloat16)
    attn_buf = jnp.zeros((rows_all, part_width), jnp.bfloat16)
    hid_buf = jnp.zeros((rows_all, part_width), jnp.bfloat16)
    inputs_all = lax.all_gather(hidden_in, "tensor", axis=1, tiled=True)
    incoming = jnp.zeros((STRETCH, width), jnp.bfloat16)
    for tick_num in range(tick_total):
        slot_num = tick_num - section_idx
        valid = (slot_num >= 0) & (slot_num < slot_total)
        slot_safe = jnp.clip(slot_num, 0, slot_total - 1)
        row_start = slot_safe * STRETCH
        first_rows = lax.dynamic_slice_in_dim(inputs_all, row_start, STRETCH, 0)
        x_full = jnp.where(section_idx == 0, first_rows, incoming)
        x_part = lax.dynamic_slice_in_dim(x_full, tensor_idx * part_width, part_width, 1)
        x_float = x_full.astype(jnp.float32)
        normed = (
            x_float
            * lax.rsqrt(jnp.mean(x_float * x_float, axis=1, keepdims=True) + eps_norm)
            * gain_vec[None, :]
        ).astype(jnp.bfloat16)
        positions = prefix + row_start + jnp.arange(STRETCH, dtype=jnp.int32)
        query_vec = jnp.dot(normed, query_w, preferred_element_type=jnp.float32).reshape(
            STRETCH, heads_local, HEAD_DIM
        )
        query_vec = rotary(query_vec, positions)
        keyval = jnp.dot(normed, keyval_w, preferred_element_type=jnp.float32)
        key_new = (
            rotary(keyval[:, :kv_width].reshape(STRETCH, kv_local, HEAD_DIM), positions)
            .astype(jnp.bfloat16)
            .reshape(STRETCH, kv_width)
        )
        value_new = keyval[:, kv_width:].astype(jnp.bfloat16)
        key_upd = lax.dynamic_update_slice(key_buf, key_new, (row_start, 0))
        value_upd = lax.dynamic_update_slice(value_buf, value_new, (row_start, 0))
        key_buf = jnp.where(valid, key_upd, key_buf)
        value_buf = jnp.where(valid, value_upd, value_buf)
        query_rows = (
            query_vec.reshape(STRETCH, kv_local, group_size, HEAD_DIM)
            .transpose(1, 0, 2, 3)
            .reshape(kv_local, STRETCH * group_size, HEAD_DIM)
        )
        row_of = row_start + jnp.arange(STRETCH * group_size, dtype=jnp.int32) // group_size
        new_keys = (
            key_upd.reshape(rows_all, kv_local, HEAD_DIM).transpose(1, 0, 2).astype(jnp.float32)
        )
        new_vals = value_upd.reshape(rows_all, kv_local, HEAD_DIM).transpose(1, 0, 2)
        new_scores = (
            jnp.einsum("kqd,kjd->kqj", query_rows, new_keys, precision=full_prec) * score_scale
        )
        new_ok = jnp.arange(rows_all, dtype=jnp.int32)[None, :] <= row_of[:, None]
        new_scores = jnp.where(new_ok[None], new_scores, masked_score)

        def kept_scores(blk_idx):
            blk_start = blk_idx * key_block
            key_tile = (
                lax.dynamic_slice_in_dim(kv_store[0], blk_start, key_block, 0)
                .reshape(key_block, kv_local, HEAD_DIM)
                .transpose(1, 0, 2)
                .astype(jnp.float32)
            )
            scores = (
                jnp.einsum("kqd,kjd->kqj", query_rows, key_tile, precision=full_prec) * score_scale
            )
            key_ok = blk_start + jnp.arange(key_block, dtype=jnp.int32) < prefix
            return jnp.where(key_ok[None, None, :], scores, masked_score)

        row_max = jnp.max(new_scores, axis=-1)
        row_sum = jnp.sum(jnp.exp(new_scores - row_max[..., None]), axis=-1)

        def stat_step(blk_idx, carry):
            run_max, run_sum = carry
            scores = kept_scores(blk_idx)
            next_max = jnp.maximum(run_max, jnp.max(scores, axis=-1))
            next_sum = run_sum * jnp.exp(run_max - next_max) + jnp.sum(
                jnp.exp(scores - next_max[..., None]), axis=-1
            )
            return (next_max, next_sum)

        row_max, row_sum = lax.fori_loop(0, block_total, stat_step, (row_max, row_sum))
        new_probs = (jnp.exp(new_scores - row_max[..., None]) / row_sum[..., None]).astype(
            jnp.bfloat16
        )
        weighted = jnp.einsum(
            "kqj,kjd->kqd", new_probs, new_vals, preferred_element_type=jnp.float32
        )

        def value_step(blk_idx, total):
            scores = kept_scores(blk_idx)
            probs = (jnp.exp(scores - row_max[..., None]) / row_sum[..., None]).astype(jnp.bfloat16)
            value_tile = (
                lax.dynamic_slice_in_dim(kv_store[1], blk_idx * key_block, key_block, 0)
                .reshape(key_block, kv_local, HEAD_DIM)
                .transpose(1, 0, 2)
            )
            return total + jnp.einsum(
                "kqj,kjd->kqd", probs, value_tile, preferred_element_type=jnp.float32
            )

        weighted = lax.fori_loop(0, block_total, value_step, weighted)
        mixed_heads = (
            weighted.reshape(kv_local, STRETCH, group_size, HEAD_DIM)
            .transpose(1, 0, 2, 3)
            .reshape(STRETCH, local_cols)
            .astype(jnp.bfloat16)
        )
        partials = jnp.dot(mixed_heads, out_w, preferred_element_type=jnp.float32)
        attn_part = lax.psum_scatter(
            partials.astype(jnp.bfloat16), "tensor", scatter_dimension=1, tiled=True
        ).astype(jnp.float32)
        hid_part = (x_part.astype(jnp.float32) + attn_part).astype(jnp.bfloat16)
        live_now = valid & (slot_num < live_count)
        attn_vals = jnp.where(live_now, attn_part.astype(jnp.bfloat16), jnp.zeros_like(hid_part))
        hid_vals = jnp.where(live_now, hid_part, jnp.zeros_like(hid_part))
        attn_buf = jnp.where(
            valid, lax.dynamic_update_slice(attn_buf, attn_vals, (row_start, 0)), attn_buf
        )
        hid_buf = jnp.where(
            valid, lax.dynamic_update_slice(hid_buf, hid_vals, (row_start, 0)), hid_buf
        )
        if tick_num + 1 < tick_total:
            joined = lax.all_gather(hid_part, "tensor", axis=1, tiled=True)
            incoming = from_behind(joined, "section", 1)
    return (attn_buf[None], hid_buf[None])


def relay_kernel(
    slots, sections, groups, tensors,
    x_in, wqkv_q, wqkv_kv, w_out, gain, kv, cos_ref, sin_ref, bias_ref,
    attn_ref, hid_ref,
    xbuf, q_send, q_recv, ss_send, ss_recv, q_own, q_cat, k_all, v_all,
    heads, p_send, p_recv, x_next, a_send, a_recv, h_recv, h_send,
    xin_s, x_r, q_s, q_r, ss_s, ss_r, h_s, h_r, p_s, p_r, xn_s, a_s, a_r, hc_s, hc_r, loc,
):
    s = lax.axis_index("section")
    g = lax.axis_index("dp")
    t = lax.axis_index("tensor")
    last = sections - 1
    per_t = groups // tensors
    width = x_next.shape[-1]
    q_cols = wqkv_q.shape[1]
    kv_cols = kv.shape[2]
    kv_heads = kv_cols // HEAD_DIM
    head_total = q_cols // HEAD_DIM
    group_size = head_total // kv_heads
    kept = kv.shape[1]
    half_cols = group_size * HEAD_DIM
    order = tuple(k for k in range(groups) if k != 2) + (2,) if groups > 2 else tuple(range(groups))

    def dev(sec, grp, ten):
        return {"section": sec, "dp": grp, "tensor": ten}

    def remote(src, dst, send, recv, target):
        return pltpu.make_async_remote_copy(
            src_ref=src, dst_ref=dst, send_sem=send, recv_sem=recv,
            device_id=target, device_id_type=pl.DeviceIdType.MESH,
        )

    barrier = pltpu.get_barrier_semaphore()
    for dg in range(groups):
        for dt in range(tensors):
            if dg or dt:
                pl.semaphore_signal(
                    barrier, inc=1,
                    device_id=dev(s, lax.rem(g + dg, groups), lax.rem(t + dt, tensors)),
                    device_id_type=pl.DeviceIdType.MESH,
                )

    @pl.when(s > 0)
    def _():
        pl.semaphore_signal(
            barrier, inc=1, device_id=dev(s - 1, g, t), device_id_type=pl.DeviceIdType.MESH
        )

    @pl.when(s < last)
    def _():
        pl.semaphore_signal(
            barrier, inc=1, device_id=dev(s + 1, g, t), device_id_type=pl.DeviceIdType.MESH
        )

    edge = jnp.where(s > 0, 1, 0) + jnp.where(s < last, 1, 0)
    pl.semaphore_wait(barrier, groups * tensors - 1 + edge)

    def input_copy(j, c, td):
        return remote(
            x_in.at[pl.ds(j * STRETCH, STRETCH), pl.ds(c * width, width)],
            xbuf.at[j, g], xin_s.at[j, c, td], x_r.at[j, g], dev(0, per_t * t + c, td),
        )

    def local_copy(j, c):
        return pltpu.make_async_copy(
            x_in.at[pl.ds(j * STRETCH, STRETCH), pl.ds(c * width, width)], xbuf.at[j, g], loc.at[j]
        )

    def for_inputs(do):
        for j in range(slots):
            for c in range(per_t):
                for td in range(tensors):
                    own = (per_t * t + c == g) & (td == t)

                    @pl.when((s == 0) & jnp.logical_not(own))
                    def _():
                        do(input_copy(j, c, td))

    for_inputs(lambda copy: copy.start())
    is_local = (s == 0) & (g // per_t == t)
    for j in range(slots):
        for c in range(per_t):

            @pl.when((s == 0) & (per_t * t + c == g))
            def _():
                local_copy(j, c).start()

    for h in range(kv_heads):
        piece = kv[0, :, h * HEAD_DIM : (h + 1) * HEAD_DIM]
        k_all[h, :kept, :HEAD_DIM] = piece
        k_all[h, :kept, HEAD_DIM:] = piece
        v_all[h, :kept, :] = kv[1, :, h * HEAD_DIM : (h + 1) * HEAD_DIM]
        fresh = k_all.shape[1] - kept
        k_all[h, kept:, :] = jnp.zeros((fresh, 2 * HEAD_DIM), jnp.bfloat16)
        v_all[h, kept:, :] = jnp.zeros((fresh, HEAD_DIM), jnp.bfloat16)
    for j in range(slots):
        for c in range(per_t):

            @pl.when((s == 0) & (per_t * t + c == g))
            def _():
                local_copy(j, c).wait()

    def q_copy(j, src, dst_slot, sem, target):
        return remote(q_send.at[j, src], q_recv.at[j, dst_slot], q_s.at[j, src], q_r.at[j, sem], target)

    def ss_copy(j, src, dst_slot, sem, target):
        return remote(
            ss_send.at[j, src], ss_recv.at[j, dst_slot], ss_s.at[j, src], ss_r.at[j, sem], target
        )

    def h_copy(j, part, slot, peer):
        cols = pl.ds(part * half_cols, half_cols)
        return remote(
            heads.at[j, slot, :, cols], heads.at[j, slot, :, cols],
            h_s.at[j, peer, part], h_r.at[j, slot, part], dev(s, peer, t),
        )

    def p_copy(j, tr):
        return remote(
            p_send.at[j, tr], p_recv.at[j, tr], p_s.at[j, tr], p_r.at[j, tr],
            dev(s, g, lax.rem(t + 1, tensors)),
        )

    def x_copy(j, tr, sec):
        return remote(x_next.at[j, tr], xbuf.at[j, tr], xn_s.at[j, tr], x_r.at[j, tr], dev(sec, g, t))

    def a_copy(j, tr, c, peer):
        return remote(a_send.at[j, tr], a_recv.at[j, c], a_s.at[j, tr], a_r.at[j, c], dev(s, peer, t))

    def hc_copy(j, sec):
        return remote(h_send.at[j], h_recv.at[j], hc_s.at[j], hc_r.at[j], dev(sec, g, t))

    def rotate(values, cosine, sine):
        return values * cosine + pltpu.roll(values, HEAD_DIM // 2, 1) * sine

    @pl.loop(0, slots)
    def _(j):
        row = pl.multiple_of(j * STRETCH, STRETCH)
        for k in order:
            d = lax.rem(g + k, groups)
            arrives = jnp.logical_not(is_local) | (d != g)

            @pl.when(arrives)
            def _():
                x_copy(j, d, s).wait_recv()

            x_val = xbuf[j, d].astype(jnp.float32)
            square = jnp.sum(x_val * x_val, axis=1, keepdims=True)
            ss_send[j, d] = jnp.broadcast_to(square, (STRETCH, HEAD_DIM))
            x_gain = (x_val * gain[...]).astype(jnp.bfloat16)
            part_q = jnp.dot(x_gain, wqkv_q[...], preferred_element_type=jnp.float32)
            part_kv = jnp.dot(x_gain, wqkv_kv[...], preferred_element_type=jnp.float32)
            if k:
                q_send[j, d, :, :q_cols] = part_q.astype(jnp.bfloat16)
                q_send[j, d, :, q_cols:] = part_kv.astype(jnp.bfloat16)
                ss_copy(j, d, g, g, dev(s, d, t)).start()
                q_copy(j, d, g, g, dev(s, d, t)).start()
            else:
                q_own[:, :q_cols] = part_q
                q_own[:, q_cols:] = part_kv
        square = ss_send[j, g]
        for k in range(1, groups):
            src = lax.rem(g + k, groups)
            ss_copy(j, src, src, src, dev(s, src, t)).wait_recv()
            q_copy(j, src, src, src, dev(s, src, t)).wait_recv()
            square = square + ss_recv[j, src]
        scale = lax.rsqrt(square * (1.0 / (groups * width)) + eps_norm)
        cosine = cos_ref[pl.ds(row, STRETCH), :]
        sine = sin_ref[pl.ds(row, STRETCH), :]

        def total(col):
            value = q_own[:, col : col + HEAD_DIM]
            for k in range(1, groups):
                src = lax.rem(g + k, groups)
                value = value + q_recv[j, src, :, col : col + HEAD_DIM].astype(jnp.float32)
            return value * scale

        for h in range(kv_heads):
            fresh = pl.ds(pl.multiple_of(kept + row, STRETCH), STRETCH)
            key_new = rotate(total(q_cols + h * HEAD_DIM), cosine, sine).astype(jnp.bfloat16)
            k_all[h, fresh, :HEAD_DIM] = key_new
            k_all[h, fresh, HEAD_DIM:] = key_new
            v_all[h, fresh, :] = total(q_cols + kv_cols + h * HEAD_DIM).astype(jnp.bfloat16)
        for h in range(head_total):
            query = rotate(total(h * HEAD_DIM), cosine, sine) * HEAD_DIM ** (-0.5)
            high = query.astype(jnp.bfloat16)
            q_cat[h, :, :HEAD_DIM] = high
            q_cat[h, :, HEAD_DIM:] = (query - high.astype(jnp.float32)).astype(jnp.bfloat16)

        for h in range(kv_heads):
            for i in range(group_size):
                n = h * group_size + i
                scores = lax.dot_general(
                    q_cat[n], k_all[h], (((1,), (1,)), ((), ())), preferred_element_type=jnp.float32
                ) + bias_ref[pl.ds(row, STRETCH), :]
                probs = jnp.exp(scores - jnp.max(scores, axis=1, keepdims=True))
                norm = jnp.sum(probs, axis=1, keepdims=True)
                mixed = jnp.dot(
                    probs.astype(jnp.bfloat16), v_all[h], preferred_element_type=jnp.float32
                )
                heads[j, g, :, n * HEAD_DIM : (n + 1) * HEAD_DIM] = (mixed / norm).astype(jnp.bfloat16)
            for k in range(1, groups):
                h_copy(j, h, g, lax.rem(g + k, groups)).start()

        for step, k in enumerate(order + (None,)):
            if k is not None:
                tr = lax.rem(g + k, groups)
                if k:
                    for h in range(kv_heads):
                        h_copy(j, h, tr, tr).wait_recv()
                p_send[j, tr] = jnp.dot(
                    heads[j, tr], w_out[...], preferred_element_type=jnp.float32
                ).astype(jnp.bfloat16)
                p_copy(j, tr).start()
            if step == 0:
                continue
            k = order[step - 1]
            tr = lax.rem(g + k, groups)
            p_copy(j, tr).wait_recv()
            attn = p_send[j, tr].astype(jnp.float32) + p_recv[j, tr].astype(jnp.float32)
            x_next[j, tr] = (xbuf[j, tr].astype(jnp.float32) + attn).astype(jnp.bfloat16)

            @pl.when(s < last)
            def _():
                x_copy(j, tr, s + 1).start()

            a_send[j, tr] = attn.astype(jnp.bfloat16)

            @pl.when(g // per_t == t)
            def _():
                if k:
                    a_copy(j, tr, lax.rem(g, per_t), tr).start()

    @pl.loop(0, slots)
    def _(j):
        rows = pl.ds(pl.multiple_of(j * STRETCH, STRETCH), STRETCH)

        @pl.when(s > 0)
        def _():
            hc_copy(j, s).wait_recv()

        for c in range(per_t):
            cols = slice(c * width, (c + 1) * width)
            owner = per_t * t + c

            @pl.when(owner != g)
            def _():
                a_copy(j, g, c, owner).wait_recv()
                attn_ref[rows, cols] = a_recv[j, c]

            @pl.when(owner == g)
            def _():
                attn_ref[rows, cols] = a_send[j, g]

            @pl.when(s == 0)
            def _():
                h_send[j, :, cols] = (
                    x_in[rows, cols].astype(jnp.float32) + attn_ref[rows, cols].astype(jnp.float32)
                ).astype(jnp.bfloat16)

            @pl.when(s > 0)
            def _():
                h_send[j, :, cols] = (
                    h_recv[j, :, cols].astype(jnp.float32)
                    + attn_ref[rows, cols].astype(jnp.float32)
                ).astype(jnp.bfloat16)

        @pl.when(s < last)
        def _():
            hc_copy(j, s + 1).start()

        hid_ref[rows, :] = h_send[j]

    for_inputs(lambda copy: copy.wait_send())

    @pl.loop(0, slots)
    def _(j):
        for k in range(groups):
            tr = lax.rem(g + k, groups)
            if k:
                q_copy(j, tr, g, g, dev(s, tr, t)).wait_send()
                ss_copy(j, tr, g, g, dev(s, tr, t)).wait_send()
                for h in range(kv_heads):
                    h_copy(j, h, g, tr).wait_send()

                @pl.when(g // per_t == t)
                def _():
                    a_copy(j, tr, lax.rem(g, per_t), tr).wait_send()

            p_copy(j, tr).wait_send()

            @pl.when(s < last)
            def _():
                x_copy(j, tr, s + 1).wait_send()

        @pl.when(s < last)
        def _():
            hc_copy(j, s + 1).wait_send()


def relay_shards(hidden_in, kv_cache, norm_gain, w_query, w_keyval, w_out, stretch_count, prefix_len):
    sections = lax.axis_size("section")
    groups = lax.axis_size("dp")
    tensors = lax.axis_size("tensor")
    width = w_query.shape[1]
    q_cols = w_query.shape[2]
    kv_store = kv_cache[0, 0]
    kept, kv_cols = kv_store.shape[1:]
    kv_heads = kv_cols // HEAD_DIM
    head_total = q_cols // HEAD_DIM
    rows_all = hidden_in.shape[0]
    slots = rows_all // STRETCH
    out_cols = hidden_in.shape[1]
    all_cols = q_cols + 2 * kv_cols
    per_t = groups // tensors
    gain = lax.dynamic_slice_in_dim(norm_gain, lax.axis_index("dp") * width, width, 1)
    prefix = prefix_len[0]
    row_idx = jnp.arange(rows_all, dtype=jnp.int32)
    half_dim = HEAD_DIM // 2
    inv_freq = theta_base ** (-(jnp.arange(half_dim, dtype=jnp.float32) * 2.0 / HEAD_DIM))
    angles = (prefix + row_idx).astype(jnp.float32)[:, None] * inv_freq[None, :]
    cosine, sine = jnp.cos(angles), jnp.sin(angles)
    cos_full = jnp.concatenate([cosine, cosine], axis=1)
    sin_full = jnp.concatenate([-sine, sine], axis=1)
    key_idx = jnp.arange(kept + rows_all, dtype=jnp.int32)[None, :]
    visible = jnp.where(key_idx < kept, key_idx < prefix, key_idx - kept <= row_idx[:, None])
    bias = jnp.where(visible, 0.0, masked_score).astype(jnp.float32)
    vmem = pl.BlockSpec(memory_space=pltpu.VMEM)
    bf16 = jnp.bfloat16
    dma = pltpu.SemaphoreType.DMA
    block = (slots, groups, STRETCH)
    attn, hid = pl.pallas_call(
        functools.partial(relay_kernel, slots, sections, groups, tensors),
        out_shape=[jax.ShapeDtypeStruct((rows_all, out_cols), bf16)] * 2,
        in_specs=[vmem] * 9,
        out_specs=[vmem] * 2,
        scratch_shapes=[
            pltpu.VMEM(block + (width,), bf16),
            pltpu.VMEM(block + (all_cols,), bf16),
            pltpu.VMEM(block + (all_cols,), bf16),
            pltpu.VMEM(block + (HEAD_DIM,), jnp.float32),
            pltpu.VMEM(block + (HEAD_DIM,), jnp.float32),
            pltpu.VMEM((STRETCH, all_cols), jnp.float32),
            pltpu.VMEM((head_total, STRETCH, 2 * HEAD_DIM), bf16),
            pltpu.VMEM((kv_heads, kept + rows_all, 2 * HEAD_DIM), bf16),
            pltpu.VMEM((kv_heads, kept + rows_all, HEAD_DIM), bf16),
            pltpu.VMEM(block + (q_cols,), bf16),
            pltpu.VMEM(block + (width,), bf16),
            pltpu.VMEM(block + (width,), bf16),
            pltpu.VMEM(block + (width,), bf16),
            pltpu.VMEM(block + (width,), bf16),
            pltpu.VMEM((slots, per_t, STRETCH, width), bf16),
            pltpu.VMEM((slots, STRETCH, out_cols), bf16),
            pltpu.VMEM((slots, STRETCH, out_cols), bf16),
            dma((slots, per_t, tensors)),
            dma((slots, groups)),
            dma((slots, groups)),
            dma((slots, groups)),
            dma((slots, groups)),
            dma((slots, groups)),
            dma((slots, groups, kv_heads)),
            dma((slots, groups, kv_heads)),
            dma((slots, groups)),
            dma((slots, groups)),
            dma((slots, groups)),
            dma((slots, groups)),
            dma((slots, per_t)),
            dma((slots,)),
            dma((slots,)),
            dma((slots,)),
        ],
        compiler_params=pltpu.CompilerParams(
            collective_id=0, has_side_effects=True, vmem_limit_bytes=60 * 2**20
        ),
    )(
        hidden_in, w_query[0], w_keyval[0].reshape(width, 2 * kv_cols), w_out[0],
        gain, kv_store, cos_full, sin_full, bias,
    )
    live = (row_idx // STRETCH < stretch_count[0])[:, None]
    return (
        jnp.where(live, attn, jnp.zeros_like(attn))[None],
        jnp.where(live, hid, jnp.zeros_like(hid))[None],
    )


def relay_fits(mesh, width, model_cols):
    return mesh.shape["tensor"] == 2 and width % HEAD_DIM == 0 and model_cols % width == 0


def solution(mesh):
    def either(hidden_in, kv_cache, norm_gain, w_query, *rest):
        fits = relay_fits(mesh, w_query.shape[1], hidden_in.shape[1])
        body = relay_shards if fits else shards
        return body(hidden_in, kv_cache, norm_gain, w_query, *rest)

    return jax.shard_map(
        either,
        mesh=mesh,
        in_specs=(
            P("dp", "tensor"),
            P("section", "dp", None, None, "tensor"),
            P("section", None),
            P("section", "dp", "tensor"),
            P("section", "dp", None, "tensor"),
            P("section", "tensor", "dp"),
            P("dp"),
            P("dp"),
        ),
        out_specs=(P("section", "dp", "tensor"), P("section", "dp", "tensor")),
        check_vma=False,
    )
```
